32 devices in a mesh: groups: 2 (over y), blk: 4 (over z), op: 2 (over x), sub: 2 (over core).
Axes of the slice: x: 2, y: 2, z: 4, core: 2. Of those that a mesh axis runs over, the one named last changes fastest.
Arguments:
- wavefunction: bfloat16 [32, 512, 512], P(('groups', 'blk'), 'sub'), parts along dimension 0, may hold values from -6 to 6
- left_ops: bfloat16 [256, 512, 512], P(('groups', 'blk', 'op'), 'sub'), parts along dimension 0, may hold values from -0.25 to 0.25
- right_ops: bfloat16 [256, 512, 512], P(('groups', 'blk', 'op'), 'sub'), parts along dimension 0, may hold values from -0.25 to 0.25
- src_local: int32 [256], P(('groups', 'blk', 'op')), parts along dimension 0, may hold values from 0 to 3
- dst_dev: int32 [256, 1], P(('groups', 'blk', 'op')), parts along dimension 0, may hold values from 0 to 3; in each aligned block of 16 rows (0 to 15, 16 to 31, ...) at most 8 rows name the same one
- dst_local: int32 [256], P(('groups', 'blk', 'op')), parts along dimension 0, may hold values from 0 to 3
- row_counts: int32 [32], P('groups'), parts along dimension 0, may hold values from 1 to 512, 4096 in all
- col_counts: int32 [32], P('groups'), parts along dimension 0, may hold values from 1 to 512, 4096 in all
Outputs:
- hpsi: float32 [32, 512, 512], P(('groups', 'blk'), 'sub', 'op'), parts along dimension 0
The draws below stay inside these ranges and needn't reach their ends.
There are 2 independent parts, one for each index of `groups`. The reference program is written for one: setup_inputs(seed, part) draws one part's arguments, and reference() takes and returns one part's arrays. A program takes and returns all parts, laid end to end along the dimension named above; each array names one. Nothing has to cross between parts.
Inputs may be any that keep to these rules, and one draw needn't show every extreme that they name: `dst_dev`: among the 16 pairs of one device at most 8 name the same blk index, and some device reaches 8. `row_counts`: they sum to 4096 and the largest is 512. `col_counts`: they sum to 4096 and the largest is 512.
All inputs are finite; a program needn't handle non-finite values.
Results may differ from the reference program's by a relative error of at most 0.0041.
Values may be sent and summed in bfloat16 or wider, within the bound.
A program may use at most 128 MiB of HBM per device.

```python
import math
import jax
import jax.numpy as jnp
import numpy as np
from jax import lax

BM = 512
BN = 512
B_DEV = 4
P_DEV = 16
CAP = 8
NBLOCKS = 16
PAIRS = 128
N_BLK = 4
N_OP = 2


def with_ends(drawn, key, least, high):
    longest = drawn.shape.index(max(drawn.shape))
    spots = []
    for shift in (0, 1):
        where = [jax.random.randint(jax.random.fold_in(key, axis), (), 0, length) for axis, length in enumerate(drawn.shape)]
        where[longest] = (where[longest] + shift) % drawn.shape[longest]
        spots.append(tuple(where))
    return drawn.at[spots[0]].set(least).at[spots[1]].set(high)


def shard_levels(rng, dims, split, least, largest):
    def one(position, shards_of):
        heights = jax.random.uniform(jax.random.fold_in(jax.random.fold_in(rng, 6), position), (shards_of,), jnp.float32, least / len(split), largest / len(split))
        return jnp.repeat(jnp.exp(heights), dims[position] // shards_of).reshape((-1,) + (1,) * (len(dims) - position - 1))

    level = one(*split[0])
    for cut in split[1:]:
        level = level * one(*cut)
    return level


def length_profile(number_of, total, limit, slope):
    weights = [(1 << 20) // math.isqrt(rank ** slope) + 1 for rank in range(2, number_of + 1)]
    spare, holding = total - limit - (number_of - 1), [1] * (number_of - 1)
    while spare > 0:
        movable = [i for i in range(number_of - 1) if holding[i] < limit]
        whole, budget = sum([weights[i] for i in movable]), spare
        for i in movable:
            addition = min(limit - holding[i], max(1, budget * weights[i] // whole), spare)
            holding[i] = holding[i] + addition
            spare = spare - addition
    return np.array([limit] + holding)


def uneven(key, amount, total, most, lean):
    if amount == 2:
        one = jax.random.randint(key, (), max(1, total - most), min(most, total - 1) + 1)
        return jnp.stack([one, total - one])
    tallies = jnp.asarray(length_profile(amount, total, most, lean), jnp.int32)
    couples = (amount - 1) // 2
    giver, sink = tallies[1:1 + 2 * couples:2], tallies[2:2 + 2 * couples:2]
    margin = jnp.minimum(giver - 1, most - sink)
    passed = jax.random.randint(jax.random.fold_in(key, 1), (couples,), 0, 1 << 20) % (margin + 1)
    tallies = tallies.at[1:1 + 2 * couples:2].set(giver - passed).at[2:2 + 2 * couples:2].set(sink + passed)
    return tallies[jax.random.permutation(jax.random.fold_in(key, 2), amount)]


def deal_out(key, own, number, rows, amount, top, limit, slope):
    sequence = jax.random.permutation(key, amount)
    heavy_load, usual = shares(amount, rows * top, limit, slope, True), shares(amount, rows * top, limit, slope, False)
    places = jnp.arange(amount)

    def named(tallies, offset_by):
        used = int((tallies > 0).sum())
        fixed = max(1, used // 4)
        moved = fixed + (places - fixed + offset_by * (used - fixed)) % max(1, amount - fixed)
        return jnp.zeros((amount,), jnp.int32).at[sequence[jnp.where(places < fixed, places, moved)]].set(jnp.asarray(tallies, jnp.int32))

    tallies = jnp.where(number % 4 == 0, named(heavy_load, number // 4), named(usual, number - number // 4 - 1))
    mixed = jax.random.permutation(jax.random.fold_in(own, 3), amount)
    donor, receiver = mixed[0:amount // 2 * 2:2], mixed[1:amount // 2 * 2:2]
    room = jnp.minimum(tallies[donor] - 1, limit - tallies[receiver]) // 2
    room = jnp.where((donor == sequence[0]) | (receiver == sequence[0]) | (tallies[receiver] == 0), 0, jnp.maximum(room, 0))
    moved = jax.random.randint(jax.random.fold_in(own, 4), (amount // 2,), 0, 1 << 20) % (room + 1)
    tallies = tallies.at[donor].add(-moved).at[receiver].add(moved)
    labels = jnp.searchsorted(jnp.cumsum(tallies), jnp.arange(rows * top), side="right").astype(jnp.int32)
    grid = labels.reshape(top, rows).T
    grid = grid[jax.random.permutation(jax.random.fold_in(own, 1), rows)]
    offset_by = jax.random.randint(jax.random.fold_in(own, 2), (rows, 1), 0, top)
    return jnp.take_along_axis(grid, (jnp.arange(top)[None, :] + offset_by) % top, axis=1)


def shares(count, total, most, skew, full):
    portions = [(1 << 20) // math.isqrt(rank ** skew) + 1 for rank in range(1, count + 1)]
    largest = most if full else min(most, max(-(-total // count), total * portions[0] // sum(portions)))
    least = 1 if total - largest >= count - 1 else 0
    counts, spare = [largest] + [least] * (count - 1), total - largest - least * (count - 1)
    while spare > 0:
        candidates = [i for i in range(1, count) if counts[i] < largest] or [i for i in range(1, count) if counts[i] < most]
        whole, remaining = sum([portions[i] for i in candidates]), spare
        for i in candidates:
            addition = min(most - counts[i], max(1, remaining * portions[i] // whole), spare)
            counts[i] = counts[i] + addition
            spare = spare - addition
    return np.array(counts)


def scatter_about(rng, shape, scale, bound, shards=(), kind=jnp.bfloat16):
    factor_of = shard_levels(rng, shape, shards, -0.22, 0.18) if shards else 1.0
    drawn = jax.random.normal(rng, shape, jnp.float32) * scale * factor_of
    return jnp.minimum(jnp.maximum(drawn, -bound), bound).astype(kind)


def setup_inputs(seed: int = 0, part: int = 0) -> dict:
    keys = jax.random.split(jax.random.key(seed), 9)
    own_keys = jax.random.split(jax.random.fold_in(keys[8], part), 9)
    wavefunction = scatter_about(own_keys[0], (NBLOCKS, BM, BN), 1.0, 6.0, ((0, 4), (1, 2)))
    left_ops = scatter_about(own_keys[1], (PAIRS, BM, BM), BM ** -0.5, 0.25, ((0, 8), (1, 2)))
    right_ops = scatter_about(own_keys[2], (PAIRS, BN, BN), BN ** -0.5, 0.25, ((0, 8), (1, 2)))
    src_local = with_ends(jax.random.randint(own_keys[3], (PAIRS,), 0, B_DEV), jax.random.fold_in(own_keys[3], 1), 0, B_DEV - 1).astype(jnp.int32)
    dst_dev_keys = jax.random.split(jax.random.fold_in(own_keys[4], 1), PAIRS // P_DEV)
    dst_dev_turns = jax.random.permutation(jax.random.fold_in(own_keys[4], 3), PAIRS // P_DEV)
    dst_dev = jax.vmap(lambda own, number: deal_out(jax.random.fold_in(own_keys[4], 2), own, number, P_DEV, N_BLK, 1, CAP, 2))(dst_dev_keys, dst_dev_turns).reshape((PAIRS, 1))
    dst_local = with_ends(jax.random.randint(own_keys[5], (PAIRS,), 0, B_DEV), jax.random.fold_in(own_keys[5], 1), 0, B_DEV - 1).astype(jnp.int32)
    row_counts = uneven(own_keys[6], NBLOCKS, NBLOCKS * BM // 2, BM, 2).astype(jnp.int32)
    col_counts = uneven(own_keys[7], NBLOCKS, NBLOCKS * BN // 2, BN, 1).astype(jnp.int32)
    return {"wavefunction": wavefunction, "left_ops": left_ops, "right_ops": right_ops, "src_local": src_local, "dst_dev": dst_dev, "dst_local": dst_local, "row_counts": row_counts, "col_counts": col_counts}


def reference(wavefunction, left_ops, right_ops, src_local, dst_dev, dst_local, row_counts, col_counts):
    row_ids = jnp.arange(BM, dtype=jnp.int32)
    col_ids = jnp.arange(BN, dtype=jnp.int32)
    keep_mask = (row_ids[None, :, None] < row_counts[:, None, None]) & (col_ids[None, None, :] < col_counts[:, None, None])
    masked = jnp.where(keep_mask, wavefunction, jnp.zeros((), wavefunction.dtype))
    pair_ids = jnp.arange(PAIRS, dtype=jnp.int32)
    sources = ((pair_ids // (P_DEV * N_OP)) * B_DEV + src_local).astype(jnp.int32)
    targets = (dst_dev[:, 0] * B_DEV + dst_local).astype(jnp.int32)
    batch_count = PAIRS // P_DEV
    packed = (left_ops.reshape(batch_count, P_DEV, BM, BM), right_ops.reshape(batch_count, P_DEV, BN, BN),
              sources.reshape(batch_count, P_DEV), targets.reshape(batch_count, P_DEV))

    def step(running, span_args):
        left_part, right_part, src_batch, dst_batch = span_args
        chosen = masked[src_batch].astype(jnp.float32)
        left_done = jnp.einsum('pik,pkj->pij', left_part.astype(jnp.float32), chosen).astype(jnp.bfloat16)
        products = jnp.einsum('pik,pck->pic', left_done.astype(jnp.float32), right_part.astype(jnp.float32)).astype(jnp.bfloat16)
        return running.at[dst_batch].add(products.astype(jnp.float32)), None

    running, unused = lax.scan(step, jnp.zeros((NBLOCKS, BM, BN), jnp.float32), packed)
    return jnp.where(keep_mask, running, jnp.zeros((), jnp.float32))
```

```python
import functools

import jax
import jax.numpy as jnp
from jax import lax
from jax.experimental import pallas as pl
from jax.experimental.pallas import tpu as pltpu
from jax.sharding import PartitionSpec as P

MESH = pl.DeviceIdType.MESH


def dest_at(step, blk, count):
    low, high = blk, count - 1 - blk
    lead = jnp.abs(high - low)
    near = jnp.minimum(low, high)
    far = jnp.where(high >= low, count - 1 - step, step)
    later = jnp.maximum(step - lead, 0)
    reach = near - later // 2
    close = jnp.where(later % 2 == 0, blk + reach, blk - reach)
    return jnp.where(step < lead, far, close)


def kernel(
    count, wave_hbm, left_hbm, right_hbm, src, dst_dev, dst_local, row_counts, col_counts, out,
    wave, left, right, runs, xs, xr, zr, zq, prev, last,
    local_sem, left_sem, own_sem, wave_send, wave_recv, right_send, right_recv,
    x_send, x_recv, z_send, z_recv, q_recv,
):
    blk, op, sub = lax.axis_index("blk"), lax.axis_index("op"), lax.axis_index("sub")
    pairs, half, width = left.shape
    blocks = wave.shape[0]
    piece = xs.shape[2]
    targets = xs.shape[0]
    has_low, has_high = blk > 0, blk < count - 1
    mine = pl.ds(pl.multiple_of(sub * half, half), half)

    wave_local = pltpu.make_async_copy(wave_hbm, wave.at[:, mine], local_sem)
    wave_local.start()

    def left_copy(p):
        return pltpu.make_async_copy(left_hbm.at[p], left.at[p], left_sem.at[p])

    def right_copy(p):
        return pltpu.make_async_copy(right_hbm.at[p], right.at[p, mine], own_sem.at[p])

    @pl.loop(0, pairs)
    def _(p):
        left_copy(p).start()
        right_copy(p).start()

    barrier = pltpu.get_barrier_semaphore()
    pl.semaphore_signal(barrier, inc=1, device_id={"sub": 1 - sub}, device_id_type=MESH)
    pl.semaphore_signal(barrier, inc=1, device_id={"op": 1 - op}, device_id_type=MESH)

    @pl.when(has_low)
    def _():
        pl.semaphore_signal(barrier, inc=1, device_id={"blk": blk - 1}, device_id_type=MESH)

    @pl.when(has_high)
    def _():
        pl.semaphore_signal(barrier, inc=1, device_id={"blk": blk + 1}, device_id_type=MESH)

    pl.semaphore_wait(barrier, 2 + has_low.astype(jnp.int32) + has_high.astype(jnp.int32))

    wave_copy = pltpu.make_async_remote_copy(
        src_ref=wave_hbm, dst_ref=wave.at[:, mine], send_sem=wave_send, recv_sem=wave_recv,
        device_id={"sub": 1 - sub}, device_id_type=MESH,
    )
    wave_copy.start()

    def right_remote(p):
        return pltpu.make_async_remote_copy(
            src_ref=right_hbm.at[p], dst_ref=right.at[p, mine],
            send_sem=right_send.at[p], recv_sem=right_recv.at[p],
            device_id={"sub": 1 - sub}, device_id_type=MESH,
        )

    @pl.loop(0, pairs)
    def _(p):
        right_remote(p).start()

    goals = [dst_dev[p] * blocks + dst_local[p] for p in range(pairs)]
    for p in range(pairs):
        found = jnp.int32(0)
        for q in range(p):
            found = jnp.where(goals[q] == goals[p], q + 1, found)
        prev[p] = found

    @pl.loop(0, targets)
    def _(t):
        found = jnp.int32(0)
        for p in range(pairs):
            found = jnp.where(goals[p] == t, p + 1, found)
        last[t] = found

    runs[0] = jnp.zeros(runs.shape[1:], jnp.float32)

    wave_local.wait()
    wave_copy.wait()

    @pl.loop(0, blocks)
    def _(j):
        at = blk * blocks + j
        shape = wave.shape[1:]
        keep = (lax.broadcasted_iota(jnp.int32, shape, 0) < row_counts[at]) & (
            lax.broadcasted_iota(jnp.int32, shape, 1) < col_counts[at]
        )
        wave[j] = jnp.where(keep, wave[j].astype(jnp.float32), 0.0).astype(wave.dtype)

    @pl.loop(0, pairs)
    def _(p):
        left_copy(p).wait()
        done = jnp.dot(left[p], wave[src[p]], preferred_element_type=jnp.float32)
        done = done.astype(jnp.bfloat16)
        right_copy(p).wait()
        right_remote(p).wait_recv()
        product = lax.dot_general(
            done, right[p], (((1,), (1,)), ((), ())), preferred_element_type=jnp.float32
        ).astype(jnp.bfloat16)
        runs[p + 1] = product.astype(jnp.float32) + runs[prev[p]]

    own_cols = pl.ds(pl.multiple_of(op * piece, piece), piece)
    peer_cols = pl.ds(pl.multiple_of((1 - op) * piece, piece), piece)

    def x_copy(t):
        return pltpu.make_async_remote_copy(
            src_ref=xs.at[t], dst_ref=xr.at[t], send_sem=x_send.at[t], recv_sem=x_recv.at[t],
            device_id={"op": 1 - op}, device_id_type=MESH,
        )

    def z_copy(t, to):
        return pltpu.make_async_remote_copy(
            src_ref=xr.at[t], dst_ref=zr.at[t], send_sem=z_send.at[t], recv_sem=z_recv.at[t],
            device_id={"blk": to}, device_id_type=MESH,
        )

    def q_copy(t, j, to):
        return pltpu.make_async_remote_copy(
            src_ref=xr.at[t], dst_ref=zq.at[j], send_sem=z_send.at[t], recv_sem=q_recv.at[j],
            device_id={"blk": to}, device_id_type=MESH,
        )

    @pl.loop(0, targets)
    def _(i):
        t = dest_at(i // blocks, blk, count) * blocks + i % blocks
        xs[t] = runs[last[t], :, peer_cols].astype(xs.dtype)
        x_copy(t).start()

    @pl.loop(0, targets - blocks)
    def _(i):
        owner = dest_at(i // blocks, blk, count)
        j = i % blocks
        t = owner * blocks + j
        x_copy(t).wait_recv()
        up = owner > blk
        follows = (up & has_low) | (jnp.logical_not(up) & has_high)

        @pl.when(follows)
        def _():
            z_copy(t, blk).wait_recv()
            xr[t] = (
                runs[last[t], :, own_cols] + xr[t].astype(jnp.float32) + zr[t].astype(jnp.float32)
            ).astype(xr.dtype)

        @pl.when(jnp.logical_not(follows))
        def _():
            xr[t] = (runs[last[t], :, own_cols] + xr[t].astype(jnp.float32)).astype(xr.dtype)

        @pl.when(up)
        def _():
            z_copy(t, blk + 1).start()

        @pl.when(owner < blk - 1)
        def _():
            z_copy(t, blk - 1).start()

        @pl.when(owner == blk - 1)
        def _():
            q_copy(t, j, blk - 1).start()

    @pl.loop(0, blocks)
    def _(j):
        t = blk * blocks + j
        x_copy(t).wait_recv()
        out[j] = runs[last[t], :, own_cols] + xr[t].astype(jnp.float32)

        @pl.when(has_low)
        def _():
            z_copy(t, blk).wait_recv()
            out[j] += zr[t].astype(jnp.float32)

        @pl.when(has_high)
        def _():
            q_copy(t, j, blk).wait_recv()
            out[j] += zq[j].astype(jnp.float32)

        shape = out.shape[1:]
        keep = (lax.broadcasted_iota(jnp.int32, shape, 0) + sub * half < row_counts[t]) & (
            lax.broadcasted_iota(jnp.int32, shape, 1) + op * piece < col_counts[t]
        )
        out[j] = jnp.where(keep, out[j], 0.0)

    @pl.loop(0, pairs)
    def _(p):
        right_remote(p).wait_send()

    @pl.loop(0, targets)
    def _(t):
        x_copy(t).wait_send()

        @pl.when(t // blocks != blk)
        def _():
            z_copy(t, blk).wait_send()


def local(wavefunction, left_ops, right_ops, src_local, dst_dev, dst_local, row_counts, col_counts):
    blocks, half, width = wavefunction.shape
    pairs = left_ops.shape[0]
    count, op_count = lax.axis_size("blk"), lax.axis_size("op")
    piece = width // op_count
    targets = count * blocks
    small = pltpu.VMEM((targets, half, piece), jnp.bfloat16)
    dma = pltpu.SemaphoreType.DMA
    return pl.pallas_call(
        functools.partial(kernel, count),
        out_shape=jax.ShapeDtypeStruct((blocks, half, piece), jnp.float32),
        in_specs=[pl.BlockSpec(memory_space=pl.ANY)] * 3 + [pl.BlockSpec(memory_space=pltpu.SMEM)] * 5,
        out_specs=pl.BlockSpec(memory_space=pltpu.VMEM),
        scratch_shapes=[
            pltpu.VMEM((blocks, 2 * half, width), jnp.bfloat16),
            pltpu.VMEM((pairs, half, width), jnp.bfloat16),
            pltpu.VMEM((pairs, 2 * half, width), jnp.bfloat16),
            pltpu.VMEM((pairs + 1, half, width), jnp.float32),
            small,
            small,
            small,
            pltpu.VMEM((blocks, half, piece), jnp.bfloat16),
            pltpu.SMEM((pairs,), jnp.int32),
            pltpu.SMEM((targets,), jnp.int32),
            dma,
            dma((pairs,)),
            dma((pairs,)),
            dma,
            dma,
            dma((pairs,)),
            dma((pairs,)),
            dma((targets,)),
            dma((targets,)),
            dma((targets,)),
            dma((targets,)),
            dma((blocks,)),
        ],
        compiler_params=pltpu.CompilerParams(
            collective_id=0, has_side_effects=True, vmem_limit_bytes=60 * 2**20
        ),
        cost_estimate=pl.CostEstimate(
            flops=4 * pairs * half * width * width * 2,
            bytes_accessed=2 * left_ops.size * 2 + 2 * wavefunction.size,
            transcendentals=0,
        ),
    )(
        wavefunction, left_ops, right_ops, src_local, dst_dev.reshape(pairs), dst_local,
        row_counts, col_counts,
    )


def solution(mesh):
    placed = (
        P(("groups", "blk"), "sub", None),
        P(("groups", "blk", "op"), "sub", None),
        P(("groups", "blk", "op"), "sub", None),
        P(("groups", "blk", "op")),
        P(("groups", "blk", "op"), None),
        P(("groups", "blk", "op")),
        P("groups"),
        P("groups"),
    )
    return jax.shard_map(
        local,
        mesh=mesh,
        in_specs=placed,
        out_specs=P(("groups", "blk"), "sub", "op"),
        check_vma=False,
    )
```

```python
import functools

import jax
import jax.numpy as jnp
from jax import lax
from jax.experimental import pallas as pl
from jax.experimental.pallas import tpu as pltpu
from jax.sharding import PartitionSpec as P

MESH = pl.DeviceIdType.MESH


TILE = 32
GROUP = 8
LAG = 2
SLOTS = 4


def kernel(
    count, op_count, chunks,
    wave_hbm, left_hbm, right_hbm, src, dst_dev, dst_local, row_counts, col_counts, out,
    wave, left, right, runs, xs, xr, zr, zl, ro, lo, stage, got, prev, last, tiles, first, tile_of, tile_row, tile_run,
    local_sem, left_sem, own_sem, wave_send, wave_recv, left_send, left_recv,
    x_send, x_recv, r_send, r_recv, l_send, l_recv, out_send, out_recv,
):
    blk, op, sub = lax.axis_index("blk"), lax.axis_index("op"), lax.axis_index("sub")
    pairs, rows, width = left.shape
    half = rows // 2
    blocks = wave.shape[0]
    targets = count * blocks
    piece = out.shape[2]
    per_half = op_count // 2
    owner = op // per_half == sub
    has_low, has_high = blk > 0, blk < count - 1
    mine = pl.ds(pl.multiple_of(sub * half, half), half)

    wave_local = pltpu.make_async_copy(wave_hbm, wave.at[:, mine], local_sem)
    wave_local.start()

    def left_copy(p):
        return pltpu.make_async_copy(left_hbm.at[p], left.at[p, mine], left_sem.at[p])

    def right_copy(p):
        return pltpu.make_async_copy(right_hbm.at[p], right.at[p], own_sem.at[p])

    @pl.loop(0, pairs)
    def _(p):
        left_copy(p).start()
        right_copy(p).start()

    barrier = pltpu.get_barrier_semaphore()
    pl.semaphore_signal(barrier, inc=1, device_id={"sub": 1 - sub}, device_id_type=MESH)
    for step in range(1, op_count):
        pl.semaphore_signal(
            barrier, inc=1, device_id={"op": lax.rem(op + step, op_count)}, device_id_type=MESH
        )

    @pl.when(has_low)
    def _():
        pl.semaphore_signal(barrier, inc=1, device_id={"blk": blk - 1}, device_id_type=MESH)

    @pl.when(has_high)
    def _():
        pl.semaphore_signal(barrier, inc=1, device_id={"blk": blk + 1}, device_id_type=MESH)

    pl.semaphore_wait(barrier, op_count + has_low.astype(jnp.int32) + has_high.astype(jnp.int32))

    wave_copy = pltpu.make_async_remote_copy(
        src_ref=wave_hbm, dst_ref=wave.at[:, mine], send_sem=wave_send, recv_sem=wave_recv,
        device_id={"sub": 1 - sub}, device_id_type=MESH,
    )
    wave_copy.start()

    def left_remote(p):
        return pltpu.make_async_remote_copy(
            src_ref=left_hbm.at[p], dst_ref=left.at[p, mine],
            send_sem=left_send.at[p], recv_sem=left_recv.at[p],
            device_id={"sub": 1 - sub}, device_id_type=MESH,
        )

    @pl.loop(0, pairs)
    def _(p):
        left_remote(p).start()

    goals = [dst_dev[p] * blocks + dst_local[p] for p in range(pairs)]
    for p in range(pairs):
        found = jnp.int32(0)
        for q in range(p):
            found = jnp.where(goals[q] == goals[p], q + 1, found)
        prev[p] = found

    first[0] = 0

    @pl.loop(0, targets)
    def _(t):
        found = jnp.int32(0)
        for p in range(pairs):
            found = jnp.where(goals[p] == t, p + 1, found)
        last[t] = found
        tiles[t] = lax.div(row_counts[t] + (TILE - 1), TILE)
        first[t + 1] = first[t] + tiles[t]

    tile_of[0] = 0
    tile_row[0] = 0

    @pl.loop(0, chunks * GROUP)
    def _(k):
        t, r = tile_of[k], tile_row[k]
        over = r + 1 >= tiles[t]
        tile_of[k + 1] = jnp.where(over, jnp.minimum(t + 1, targets - 1), t)
        tile_row[k + 1] = jnp.where(over, 0, r + 1)
        tile_run[k] = last[t]

    runs[0] = jnp.zeros(runs.shape[1:], jnp.float32)

    wave_local.wait()
    wave_copy.wait()

    @pl.loop(0, blocks)
    def _(j):
        at = blk * blocks + j
        shape = wave.shape[1:]
        keep = (lax.broadcasted_iota(jnp.int32, shape, 0) < row_counts[at]) & (
            lax.broadcasted_iota(jnp.int32, shape, 1) < col_counts[at]
        )
        wave[j] = jnp.where(keep, wave[j].astype(jnp.float32), 0.0).astype(wave.dtype)

    @pl.loop(0, pairs)
    def _(p):
        left_copy(p).wait()
        left_remote(p).wait_recv()
        done = jnp.dot(left[p], wave[src[p]], preferred_element_type=jnp.float32)
        done = done.astype(jnp.bfloat16)
        right_copy(p).wait()
        product = lax.dot_general(
            done, right[p], (((1,), (1,)), ((), ())), preferred_element_type=jnp.float32
        ).astype(jnp.bfloat16)
        runs[p + 1] = product.astype(jnp.float32).reshape(runs.shape[1:]) + runs[prev[p]]

    def chunk_tiles(c):
        return pl.ds(c * GROUP, GROUP)

    def x_copy(h, c):
        to = sub * per_half + h
        slot = lax.rem(op - to + op_count - 1 + op_count, op_count)
        return pltpu.make_async_remote_copy(
            src_ref=xs.at[h, chunk_tiles(c)], dst_ref=xr.at[slot, chunk_tiles(c)],
            send_sem=x_send.at[h, c], recv_sem=x_recv.at[slot, c],
            device_id={"op": to}, device_id_type=MESH,
        )

    def x_wait(slot, c):
        pltpu.make_async_remote_copy(
            src_ref=xs.at[0, chunk_tiles(c)], dst_ref=xr.at[slot, chunk_tiles(c)],
            send_sem=x_send.at[0, c], recv_sem=x_recv.at[slot, c],
            device_id={"op": op}, device_id_type=MESH,
        ).wait_recv()

    def r_copy(c):
        return pltpu.make_async_remote_copy(
            src_ref=ro.at[lax.rem(c, SLOTS)], dst_ref=zr.at[chunk_tiles(c)],
            send_sem=r_send.at[c], recv_sem=r_recv.at[c],
            device_id={"blk": blk + 1}, device_id_type=MESH,
        )

    def l_copy(c):
        return pltpu.make_async_remote_copy(
            src_ref=lo.at[lax.rem(c, SLOTS)], dst_ref=zl.at[chunk_tiles(c)],
            send_sem=l_send.at[c], recv_sem=l_recv.at[c],
            device_id={"blk": blk - 1}, device_id_type=MESH,
        )

    def out_copy(j):
        return pltpu.make_async_remote_copy(
            src_ref=stage.at[j], dst_ref=got.at[j], send_sem=out_send.at[j], recv_sem=out_recv.at[j],
            device_id={"sub": 1 - sub}, device_id_type=MESH,
        )

    def send_chunk(c):
        for q in range(GROUP):
            k = c * GROUP + q
            for h in range(per_half):
                part = runs[tile_run[k], tile_row[k], :, h * piece:(h + 1) * piece]
                xs[h, k] = part.astype(xs.dtype)
        for h in range(per_half):

            @pl.when(sub * per_half + h != op)
            def _():
                x_copy(h, c).start()

    if op_count > 2:
        pl.loop(0, chunks)(send_chunk)
    else:

        @pl.when(jnp.logical_not(owner))
        def _():
            pl.loop(0, chunks)(send_chunk)

    def add_chunk(c):
        for slot in range(op_count - 1):
            x_wait(slot, c)
        own = pl.ds(pl.multiple_of(lax.rem(op, per_half) * piece, piece), piece)
        for q in range(GROUP):
            k = c * GROUP + q
            total = runs[tile_run[k], tile_row[k], :, own]
            for slot in range(op_count - 1):
                total += xr[slot, k].astype(jnp.float32)
            xr[0, k] = total.astype(xr.dtype)

    def pass_on(c, has_in, has_out, copy, arrived, slots):
        @pl.when((c >= 0) & (c < chunks))
        def _():
            @pl.when(has_in)
            def _():
                copy(c).wait_recv()

            @pl.when(has_out)
            def _():
                @pl.when(c >= SLOTS)
                def _():
                    copy(c - SLOTS).wait_send()

                @pl.when(has_in)
                def _():
                    slots[lax.rem(c, SLOTS)] = (
                        xr[0, chunk_tiles(c)].astype(jnp.float32)
                        + arrived[chunk_tiles(c)].astype(jnp.float32)
                    ).astype(slots.dtype)

                @pl.when(jnp.logical_not(has_in))
                def _():
                    slots[lax.rem(c, SLOTS)] = xr[0, chunk_tiles(c)]

                copy(c).start()

    def finish(j, side):
        t = blk * blocks + j
        for r in range(half // TILE):
            row = side * (half // TILE) + r
            at = jnp.minimum(first[t] + row, chunks * GROUP - 1)
            total = xr[0, at].astype(jnp.float32)
            total += jnp.where(has_low, zr[at].astype(jnp.float32), 0.0)
            total += jnp.where(has_high, zl[at].astype(jnp.float32), 0.0)
            shape = total.shape
            keep = (lax.broadcasted_iota(jnp.int32, shape, 0) + row * TILE < row_counts[t]) & (
                lax.broadcasted_iota(jnp.int32, shape, 1) + op * piece < col_counts[t]
            )
            yield r, jnp.where(keep, total, 0.0)

    @pl.when(owner)
    def _():
        @pl.loop(0, chunks + LAG * (count - 1))
        def _(i):
            @pl.when(i < chunks)
            def _():
                add_chunk(i)

            pass_on(i - LAG * blk, has_low, has_high, r_copy, zr, ro)
            pass_on(i - LAG * (count - 1 - blk), has_high, has_low, l_copy, zl, lo)

        @pl.loop(0, blocks)
        def _(j):
            for r, total in finish(j, 1 - sub):
                stage[j, r * TILE:(r + 1) * TILE] = total
            out_copy(j).start()

        @pl.loop(0, blocks)
        def _(j):
            for r, total in finish(j, sub):
                out[j, r * TILE:(r + 1) * TILE] = total

        @pl.loop(chunks - SLOTS, chunks)
        def _(c):
            @pl.when(has_high)
            def _():
                r_copy(c).wait_send()

            @pl.when(has_low)
            def _():
                l_copy(c).wait_send()

        @pl.loop(0, blocks)
        def _(j):
            out_copy(j).wait_send()

    @pl.when(jnp.logical_not(owner))
    def _():
        @pl.loop(0, blocks)
        def _(j):
            out_copy(j).wait_recv()
            out[j] = got[j]

    @pl.loop(0, pairs)
    def _(p):
        left_remote(p).wait_send()

    for h in range(per_half):

        @pl.when(sub * per_half + h != op)
        def _():
            @pl.loop(0, chunks)
            def _(c):
                x_copy(h, c).wait_send()


def local(wavefunction, left_ops, right_ops, src_local, dst_dev, dst_local, row_counts, col_counts):
    blocks, half, width = wavefunction.shape
    rows = 2 * half
    pairs = left_ops.shape[0]
    count, op_count = lax.axis_size("blk"), lax.axis_size("op")
    piece = width // op_count
    targets = count * blocks
    most = (targets * rows // 2 + targets * (TILE - 1)) // TILE
    chunks = -(-most // GROUP)
    packed = chunks * GROUP
    dma = pltpu.SemaphoreType.DMA
    bf16 = jnp.bfloat16
    return pl.pallas_call(
        functools.partial(kernel, count, op_count, chunks),
        out_shape=jax.ShapeDtypeStruct((blocks, half, piece), jnp.float32),
        in_specs=[pl.BlockSpec(memory_space=pl.ANY)] * 3 + [pl.BlockSpec(memory_space=pltpu.SMEM)] * 5,
        out_specs=pl.BlockSpec(memory_space=pltpu.VMEM),
        scratch_shapes=[
            pltpu.VMEM((blocks, rows, width), bf16),
            pltpu.VMEM((pairs, rows, width), bf16),
            pltpu.VMEM((pairs, half, width), bf16),
            pltpu.VMEM((pairs + 1, rows // TILE, TILE, width // 2), jnp.float32),
            pltpu.VMEM((op_count // 2, packed, TILE, piece), bf16),
            pltpu.VMEM((op_count - 1, packed, TILE, piece), bf16),
            pltpu.VMEM((packed, TILE, piece), bf16),
            pltpu.VMEM((packed, TILE, piece), bf16),
            pltpu.VMEM((SLOTS, GROUP, TILE, piece), bf16),
            pltpu.VMEM((SLOTS, GROUP, TILE, piece), bf16),
            pltpu.VMEM((blocks, half, piece), jnp.float32),
            pltpu.VMEM((blocks, half, piece), jnp.float32),
            pltpu.SMEM((pairs,), jnp.int32),
            pltpu.SMEM((targets,), jnp.int32),
            pltpu.SMEM((targets,), jnp.int32),
            pltpu.SMEM((targets + 1,), jnp.int32),
            pltpu.SMEM((chunks * GROUP + 1,), jnp.int32),
            pltpu.SMEM((chunks * GROUP + 1,), jnp.int32),
            pltpu.SMEM((chunks * GROUP,), jnp.int32),
            dma,
            dma((pairs,)),
            dma((pairs,)),
            dma,
            dma,
            dma((pairs,)),
            dma((pairs,)),
            dma((op_count // 2, chunks)),
            dma((op_count - 1, chunks)),
            dma((chunks,)),
            dma((chunks,)),
            dma((chunks,)),
            dma((chunks,)),
            dma((blocks,)),
            dma((blocks,)),
        ],
        compiler_params=pltpu.CompilerParams(
            collective_id=0, has_side_effects=True, vmem_limit_bytes=60 * 2**20
        ),
        cost_estimate=pl.CostEstimate(
            flops=6 * pairs * half * width * width * 2,
            bytes_accessed=2 * left_ops.size * 2 + 2 * wavefunction.size,
            transcendentals=0,
        ),
    )(
        wavefunction, left_ops, right_ops, src_local, dst_dev.reshape(pairs), dst_local,
        row_counts, col_counts,
    )


def solution(mesh):
    placed = (
        P(("groups", "blk"), "sub", None),
        P(("groups", "blk", "op"), "sub", None),
        P(("groups", "blk", "op"), "sub", None),
        P(("groups", "blk", "op")),
        P(("groups", "blk", "op"), None),
        P(("groups", "blk", "op")),
        P("groups"),
        P("groups"),
    )
    return jax.shard_map(
        local,
        mesh=mesh,
        in_specs=placed,
        out_specs=P(("groups", "blk"), "sub", "op"),
        check_vma=False,
    )
```

```python
import functools

import jax
import jax.numpy as jnp
from jax import lax
from jax.experimental import pallas as pl
from jax.experimental.pallas import tpu as pltpu
from jax.sharding import PartitionSpec as P

MESH = pl.DeviceIdType.MESH


TILE = 32
GROUP = 8
SKEW = 3
AHEAD = 10
SLOTS = 4


def kernel(
    count, op_count, chunks,
    wave_hbm, left_hbm, right_hbm, src, dst_dev, dst_local, row_counts, col_counts, out,
    wave, done, right, runs, xs, xr, zin, zout, stage, got, prev, last, tiles, first, tile_of, tile_row, tile_run,
    local_sem, left_sem, own_sem, wave_send, wave_recv, done_send, done_recv,
    x_send, x_recv, t_send, t_recv, z_send, z_recv, out_send, out_recv,
):
    blk, op, sub = lax.axis_index("blk"), lax.axis_index("op"), lax.axis_index("sub")
    pairs, half, width = right.shape
    blocks = wave.shape[0]
    targets = count * blocks
    piece = out.shape[2]
    per_half = op_count // 2
    owner = op // per_half == sub
    has_low, has_high = blk > 0, blk < count - 1
    mine = pl.ds(pl.multiple_of(sub * half, half), half)

    wave_local = pltpu.make_async_copy(wave_hbm, wave.at[:, mine], local_sem)
    wave_local.start()

    def left_copy(p):
        return pltpu.make_async_copy(left_hbm.at[p], done.at[p, mine], left_sem.at[p])

    def right_copy(p):
        return pltpu.make_async_copy(right_hbm.at[p], right.at[p], own_sem.at[p])

    @pl.loop(0, pairs)
    def _(p):
        left_copy(p).start()
        right_copy(p).start()

    barrier = pltpu.get_barrier_semaphore()
    pl.semaphore_signal(barrier, inc=1, device_id={"sub": 1 - sub}, device_id_type=MESH)
    for step in range(1, op_count):
        pl.semaphore_signal(
            barrier, inc=1, device_id={"op": lax.rem(op + step, op_count)}, device_id_type=MESH
        )

    @pl.when(has_low)
    def _():
        pl.semaphore_signal(barrier, inc=1, device_id={"blk": blk - 1}, device_id_type=MESH)

    @pl.when(has_high)
    def _():
        pl.semaphore_signal(barrier, inc=1, device_id={"blk": blk + 1}, device_id_type=MESH)

    pl.semaphore_wait(barrier, op_count + has_low.astype(jnp.int32) + has_high.astype(jnp.int32))

    wave_copy = pltpu.make_async_remote_copy(
        src_ref=wave_hbm, dst_ref=wave.at[:, mine], send_sem=wave_send, recv_sem=wave_recv,
        device_id={"sub": 1 - sub}, device_id_type=MESH,
    )
    wave_copy.start()

    def done_copy(p):
        return pltpu.make_async_remote_copy(
            src_ref=done.at[p, mine], dst_ref=done.at[p, mine],
            send_sem=done_send.at[p], recv_sem=done_recv.at[p],
            device_id={"sub": 1 - sub}, device_id_type=MESH,
        )

    goals = [dst_dev[p] * blocks + dst_local[p] for p in range(pairs)]
    for p in range(pairs):
        found = jnp.int32(0)
        for q in range(p):
            found = jnp.where(goals[q] == goals[p], q + 1, found)
        prev[p] = found

    first[0] = 0

    @pl.loop(0, targets)
    def _(t):
        found = jnp.int32(0)
        for p in range(pairs):
            found = jnp.where(goals[p] == t, p + 1, found)
        last[t] = found
        tiles[t] = lax.div(row_counts[t] + (TILE - 1), TILE)
        first[t + 1] = first[t] + tiles[t]

    tile_of[0] = 0
    tile_row[0] = 0

    @pl.loop(0, chunks * GROUP)
    def _(k):
        t, r = tile_of[k], tile_row[k]
        over = r + 1 >= tiles[t]
        tile_of[k + 1] = jnp.where(over, jnp.minimum(t + 1, targets - 1), t)
        tile_row[k + 1] = jnp.where(over, 0, r + 1)
        tile_run[k] = last[t]

    runs[0] = jnp.zeros(runs.shape[1:], jnp.float32)

    wave_local.wait()
    wave_copy.wait()

    @pl.loop(0, blocks)
    def _(j):
        at = blk * blocks + j
        shape = wave.shape[1:]
        keep = (lax.broadcasted_iota(jnp.int32, shape, 0) < row_counts[at]) & (
            lax.broadcasted_iota(jnp.int32, shape, 1) < col_counts[at]
        )
        wave[j] = jnp.where(keep, wave[j].astype(jnp.float32), 0.0).astype(wave.dtype)

    @pl.loop(0, pairs)
    def _(p):
        left_copy(p).wait()
        part = jnp.dot(done[p, mine], wave[src[p]], preferred_element_type=jnp.float32)
        done[p, mine] = part.astype(done.dtype)
        done_copy(p).start()

    @pl.loop(0, pairs)
    def _(p):
        right_copy(p).wait()
        done_copy(p).wait_recv()
        product = lax.dot_general(
            done[p], right[p], (((1,), (1,)), ((), ())), preferred_element_type=jnp.float32
        ).astype(jnp.bfloat16)
        runs[p + 1] = product.astype(jnp.float32).reshape(runs.shape[1:]) + runs[prev[p]]

    def chunk_tiles(c):
        return pl.ds(c * GROUP, GROUP)

    def x_copy(h, c):
        to = sub * per_half + h
        slot = lax.rem(op - to + op_count - 1 + op_count, op_count)
        return pltpu.make_async_remote_copy(
            src_ref=xs.at[h, chunk_tiles(c)], dst_ref=xr.at[slot, chunk_tiles(c)],
            send_sem=x_send.at[h, c], recv_sem=x_recv.at[slot, c],
            device_id={"op": to}, device_id_type=MESH,
        )

    def x_wait(slot, c):
        pltpu.make_async_remote_copy(
            src_ref=xs.at[0, chunk_tiles(c)], dst_ref=xr.at[slot, chunk_tiles(c)],
            send_sem=x_send.at[0, c], recv_sem=x_recv.at[slot, c],
            device_id={"op": op}, device_id_type=MESH,
        ).wait_recv()

    def t_copy(c):
        return pltpu.make_async_remote_copy(
            src_ref=xr.at[0, chunk_tiles(c)], dst_ref=xr.at[0, chunk_tiles(c)],
            send_sem=t_send.at[c], recv_sem=t_recv.at[c],
            device_id={"sub": 1 - sub}, device_id_type=MESH,
        )

    def z_copy(c, to):
        return pltpu.make_async_remote_copy(
            src_ref=zout.at[lax.rem(c, SLOTS)], dst_ref=zin.at[chunk_tiles(c)],
            send_sem=z_send.at[c], recv_sem=z_recv.at[c],
            device_id={"blk": to}, device_id_type=MESH,
        )

    def out_copy(j):
        return pltpu.make_async_remote_copy(
            src_ref=stage.at[j], dst_ref=got.at[j], send_sem=out_send.at[j], recv_sem=out_recv.at[j],
            device_id={"sub": 1 - sub}, device_id_type=MESH,
        )

    def send_chunk(c):
        for q in range(GROUP):
            k = c * GROUP + q
            for h in range(per_half):
                part = runs[tile_run[k], tile_row[k], :, h * piece:(h + 1) * piece]
                xs[h, k] = part.astype(xs.dtype)
        for h in range(per_half):

            @pl.when(sub * per_half + h != op)
            def _():
                x_copy(h, c).start()

    def add_chunk(c):
        for slot in range(op_count - 1):
            x_wait(slot, c)
        own = pl.ds(pl.multiple_of(lax.rem(op, per_half) * piece, piece), piece)
        for q in range(GROUP):
            k = c * GROUP + q
            total = runs[tile_run[k], tile_row[k], :, own]
            for slot in range(op_count - 1):
                total += xr[slot, k].astype(jnp.float32)
            xr[0, k] = total.astype(xr.dtype)
        t_copy(c).start()

    def pass_on(c, has_in, has_out, to):
        @pl.when(has_in)
        def _():
            z_copy(c, to).wait_recv()

        @pl.when(has_out)
        def _():
            @pl.when(c >= SLOTS)
            def _():
                z_copy(c - SLOTS, to).wait_send()

            @pl.when(has_in)
            def _():
                zout[lax.rem(c, SLOTS)] = (
                    xr[0, chunk_tiles(c)].astype(jnp.float32)
                    + zin[chunk_tiles(c)].astype(jnp.float32)
                ).astype(zout.dtype)

            @pl.when(jnp.logical_not(has_in))
            def _():
                zout[lax.rem(c, SLOTS)] = xr[0, chunk_tiles(c)]

            z_copy(c, to).start()

    def finish(has_in, has_got, has_out, to):
        def tile(j, row):
            return jnp.minimum(first[blk * blocks + j] + row, chunks * GROUP - 1)

        steps = half // TILE

        @pl.when(has_in)
        def _():
            @pl.loop(0, blocks)
            def _(j):
                for r in range(steps):
                    stage[j, r * TILE:(r + 1) * TILE] = zin[tile(j, (1 - sub) * steps + r)]
                out_copy(j).start()

        @pl.loop(0, blocks)
        def _(j):
            @pl.when(has_got)
            def _():
                out_copy(j).wait_recv()

            t = blk * blocks + j
            for r in range(steps):
                row = sub * steps + r
                total = xr[0, tile(j, row)].astype(jnp.float32)
                total += jnp.where(has_in, zin[tile(j, row)].astype(jnp.float32), 0.0)
                given = got[j, r * TILE:(r + 1) * TILE].astype(jnp.float32)
                total += jnp.where(has_got, given, 0.0)
                shape = total.shape
                keep = (
                    lax.broadcasted_iota(jnp.int32, shape, 0) + row * TILE < row_counts[t]
                ) & (lax.broadcasted_iota(jnp.int32, shape, 1) + op * piece < col_counts[t])
                out[j, r * TILE:(r + 1) * TILE] = jnp.where(keep, total, 0.0)

        @pl.when(has_in)
        def _():
            @pl.loop(0, blocks)
            def _(j):
                out_copy(j).wait_send()

        @pl.when(has_out)
        def _():
            @pl.loop(chunks - SLOTS, chunks)
            def _(c):
                z_copy(c, to).wait_send()

    @pl.when(owner)
    def _():
        if op_count > 2:
            pl.loop(0, chunks)(send_chunk)

        @pl.loop(0, chunks + SKEW * (count - 1))
        def _(i):
            @pl.when(i < chunks)
            def _():
                add_chunk(i)

            c = i - SKEW * blk

            @pl.when((c >= 0) & (c < chunks))
            def _():
                pass_on(c, has_low, has_high, blk + 1)

        finish(has_low, has_high, has_high, blk + 1)

        @pl.loop(0, chunks)
        def _(c):
            t_copy(c).wait_send()

    @pl.when(jnp.logical_not(owner))
    def _():
        @pl.loop(0, chunks + AHEAD)
        def _(i):
            @pl.when(i < chunks)
            def _():
                send_chunk(i)

            @pl.when(i >= AHEAD)
            def _():
                t_copy(i - AHEAD).wait_recv()
                pass_on(i - AHEAD, has_high, has_low, blk - 1)

        finish(has_high, has_low, has_low, blk - 1)

    @pl.loop(0, pairs)
    def _(p):
        done_copy(p).wait_send()

    for h in range(per_half):

        @pl.when(sub * per_half + h != op)
        def _():
            @pl.loop(0, chunks)
            def _(c):
                x_copy(h, c).wait_send()


def local(wavefunction, left_ops, right_ops, src_local, dst_dev, dst_local, row_counts, col_counts):
    blocks, half, width = wavefunction.shape
    rows = 2 * half
    pairs = left_ops.shape[0]
    count, op_count = lax.axis_size("blk"), lax.axis_size("op")
    piece = width // op_count
    targets = count * blocks
    most = (targets * rows // 2 + targets * (TILE - 1)) // TILE
    chunks = -(-most // GROUP)
    packed = chunks * GROUP
    dma = pltpu.SemaphoreType.DMA
    bf16 = jnp.bfloat16
    return pl.pallas_call(
        functools.partial(kernel, count, op_count, chunks),
        out_shape=jax.ShapeDtypeStruct((blocks, half, piece), jnp.float32),
        in_specs=[pl.BlockSpec(memory_space=pl.ANY)] * 3 + [pl.BlockSpec(memory_space=pltpu.SMEM)] * 5,
        out_specs=pl.BlockSpec(memory_space=pltpu.VMEM),
        scratch_shapes=[
            pltpu.VMEM((blocks, rows, width), bf16),
            pltpu.VMEM((pairs, rows, width), bf16),
            pltpu.VMEM((pairs, half, width), bf16),
            pltpu.VMEM((pairs + 1, rows // TILE, TILE, width // 2), jnp.float32),
            pltpu.VMEM((op_count // 2, packed, TILE, piece), bf16),
            pltpu.VMEM((op_count - 1, packed, TILE, piece), bf16),
            pltpu.VMEM((packed, TILE, piece), bf16),
            pltpu.VMEM((SLOTS, GROUP, TILE, piece), bf16),
            pltpu.VMEM((blocks, half, piece), bf16),
            pltpu.VMEM((blocks, half, piece), bf16),
            pltpu.SMEM((pairs,), jnp.int32),
            pltpu.SMEM((targets,), jnp.int32),
            pltpu.SMEM((targets,), jnp.int32),
            pltpu.SMEM((targets + 1,), jnp.int32),
            pltpu.SMEM((chunks * GROUP + 1,), jnp.int32),
            pltpu.SMEM((chunks * GROUP + 1,), jnp.int32),
            pltpu.SMEM((chunks * GROUP,), jnp.int32),
            dma,
            dma((pairs,)),
            dma((pairs,)),
            dma,
            dma,
            dma((pairs,)),
            dma((pairs,)),
            dma((op_count // 2, chunks)),
            dma((op_count - 1, chunks)),
            dma((chunks,)),
            dma((chunks,)),
            dma((chunks,)),
            dma((chunks,)),
            dma((blocks,)),
            dma((blocks,)),
        ],
        compiler_params=pltpu.CompilerParams(
            collective_id=0, has_side_effects=True, vmem_limit_bytes=60 * 2**20
        ),
        cost_estimate=pl.CostEstimate(
            flops=4 * pairs * half * width * width * 2,
            bytes_accessed=2 * left_ops.size * 2 + 2 * wavefunction.size,
            transcendentals=0,
        ),
    )(
        wavefunction, left_ops, right_ops, src_local, dst_dev.reshape(pairs), dst_local,
        row_counts, col_counts,
    )


def solution(mesh):
    placed = (
        P(("groups", "blk"), "sub", None),
        P(("groups", "blk", "op"), "sub", None),
        P(("groups", "blk", "op"), "sub", None),
        P(("groups", "blk", "op")),
        P(("groups", "blk", "op"), None),
        P(("groups", "blk", "op")),
        P("groups"),
        P("groups"),
    )
    return jax.shard_map(
        local,
        mesh=mesh,
        in_specs=placed,
        out_specs=P(("groups", "blk"), "sub", "op"),
        check_vma=False,
    )
```

```python
import functools

import jax
import jax.numpy as jnp
from jax import lax
from jax.experimental import pallas as pl
from jax.experimental.pallas import tpu as pltpu
from jax.sharding import PartitionSpec as P

MESH = pl.DeviceIdType.MESH


TILE = 16
GROUP = 8
SKEW = 6
AHEAD = 20
SLOTS = 8


def kernel(
    count, op_count, chunks,
    wave_hbm, left_hbm, right_hbm, src, dst_dev, dst_local, row_counts, col_counts, out,
    wave, done, right, runs, xs, xr, zin, zout, stage, got, prev, last, tiles, first, tile_of, tile_row, tile_run,
    local_sem, left_sem, own_sem, wave_send, wave_recv, done_send, done_recv,
    x_send, x_recv, t_send, t_recv, z_send, z_recv, out_send, out_recv,
):
    blk, op, sub = lax.axis_index("blk"), lax.axis_index("op"), lax.axis_index("sub")
    pairs, half, width = right.shape
    blocks = wave.shape[0]
    targets = count * blocks
    piece = out.shape[2]
    per_half = op_count // 2
    owner = op // per_half == sub
    has_low, has_high = blk > 0, blk < count - 1
    mine = pl.ds(pl.multiple_of(sub * half, half), half)

    wave_local = pltpu.make_async_copy(wave_hbm, wave.at[:, mine], local_sem)
    wave_local.start()

    def left_copy(p):
        return pltpu.make_async_copy(left_hbm.at[p], done.at[p, mine], left_sem.at[p])

    def right_copy(p):
        return pltpu.make_async_copy(right_hbm.at[p], right.at[p], own_sem.at[p])

    @pl.loop(0, pairs)
    def _(p):
        left_copy(p).start()

    @pl.loop(0, pairs)
    def _(p):
        right_copy(p).start()

    barrier = pltpu.get_barrier_semaphore()
    pl.semaphore_signal(barrier, inc=1, device_id={"sub": 1 - sub}, device_id_type=MESH)
    for step in range(1, op_count):
        pl.semaphore_signal(
            barrier, inc=1, device_id={"op": lax.rem(op + step, op_count)}, device_id_type=MESH
        )

    @pl.when(has_low)
    def _():
        pl.semaphore_signal(barrier, inc=1, device_id={"blk": blk - 1}, device_id_type=MESH)

    @pl.when(has_high)
    def _():
        pl.semaphore_signal(barrier, inc=1, device_id={"blk": blk + 1}, device_id_type=MESH)

    pl.semaphore_wait(barrier, op_count + has_low.astype(jnp.int32) + has_high.astype(jnp.int32))

    wave_copy = pltpu.make_async_remote_copy(
        src_ref=wave_hbm, dst_ref=wave.at[:, mine], send_sem=wave_send, recv_sem=wave_recv,
        device_id={"sub": 1 - sub}, device_id_type=MESH,
    )
    wave_copy.start()

    def done_copy(p):
        return pltpu.make_async_remote_copy(
            src_ref=done.at[p, mine], dst_ref=done.at[p, mine],
            send_sem=done_send.at[p], recv_sem=done_recv.at[p],
            device_id={"sub": 1 - sub}, device_id_type=MESH,
        )

    goals = [dst_dev[p] * blocks + dst_local[p] for p in range(pairs)]
    for p in range(pairs):
        found = jnp.int32(0)
        for q in range(p):
            found = jnp.where(goals[q] == goals[p], q + 1, found)
        prev[p] = found

    first[0] = 0

    @pl.loop(0, targets)
    def _(t):
        found = jnp.int32(0)
        for p in range(pairs):
            found = jnp.where(goals[p] == t, p + 1, found)
        last[t] = found
        tiles[t] = lax.div(row_counts[t] + (TILE - 1), TILE)
        first[t + 1] = first[t] + tiles[t]

    tile_of[0] = 0
    tile_row[0] = 0

    @pl.loop(0, chunks * GROUP)
    def _(k):
        t, r = tile_of[k], tile_row[k]
        over = r + 1 >= tiles[t]
        tile_of[k + 1] = jnp.where(over, jnp.minimum(t + 1, targets - 1), t)
        tile_row[k + 1] = jnp.where(over, 0, r + 1)
        tile_run[k] = last[t]

    runs[0] = jnp.zeros(runs.shape[1:], jnp.float32)

    wave_local.wait()
    wave_copy.wait()

    @pl.loop(0, blocks)
    def _(j):
        at = blk * blocks + j
        shape = wave.shape[1:]
        keep = (lax.broadcasted_iota(jnp.int32, shape, 0) < row_counts[at]) & (
            lax.broadcasted_iota(jnp.int32, shape, 1) < col_counts[at]
        )
        wave[j] = jnp.where(keep, wave[j].astype(jnp.float32), 0.0).astype(wave.dtype)

    @pl.loop(0, pairs)
    def _(p):
        left_copy(p).wait()
        part = jnp.dot(done[p, mine], wave[src[p]], preferred_element_type=jnp.float32)
        done[p, mine] = part.astype(done.dtype)
        done_copy(p).start()

    @pl.loop(0, pairs)
    def _(p):
        right_copy(p).wait()
        done_copy(p).wait_recv()
        for side in range(2):
            product = lax.dot_general(
                done[p, side * half:(side + 1) * half], right[p], (((1,), (1,)), ((), ())),
                preferred_element_type=jnp.float32,
            ).astype(jnp.bfloat16)
            part = product.astype(jnp.float32).reshape((half // TILE,) + runs.shape[2:])
            at = pl.ds(side * (half // TILE), half // TILE)
            runs[p + 1, at] = part + runs[prev[p], at]

    def chunk_tiles(c):
        return pl.ds(c * GROUP, GROUP)

    def x_copy(h, c):
        to = sub * per_half + h
        slot = lax.rem(op - to + op_count - 1 + op_count, op_count)
        return pltpu.make_async_remote_copy(
            src_ref=xs.at[h, chunk_tiles(c)], dst_ref=xr.at[slot, chunk_tiles(c)],
            send_sem=x_send.at[h, c], recv_sem=x_recv.at[slot, c],
            device_id={"op": to}, device_id_type=MESH,
        )

    def x_wait(slot, c):
        pltpu.make_async_remote_copy(
            src_ref=xs.at[0, chunk_tiles(c)], dst_ref=xr.at[slot, chunk_tiles(c)],
            send_sem=x_send.at[0, c], recv_sem=x_recv.at[slot, c],
            device_id={"op": op}, device_id_type=MESH,
        ).wait_recv()

    def t_copy(c):
        return pltpu.make_async_remote_copy(
            src_ref=xr.at[0, chunk_tiles(c)], dst_ref=xr.at[0, chunk_tiles(c)],
            send_sem=t_send.at[c], recv_sem=t_recv.at[c],
            device_id={"sub": 1 - sub}, device_id_type=MESH,
        )

    def z_copy(c, to):
        return pltpu.make_async_remote_copy(
            src_ref=zout.at[lax.rem(c, SLOTS)], dst_ref=zin.at[chunk_tiles(c)],
            send_sem=z_send.at[c], recv_sem=z_recv.at[c],
            device_id={"blk": to}, device_id_type=MESH,
        )

    def out_copy(j):
        return pltpu.make_async_remote_copy(
            src_ref=stage.at[j], dst_ref=got.at[j], send_sem=out_send.at[j], recv_sem=out_recv.at[j],
            device_id={"sub": 1 - sub}, device_id_type=MESH,
        )

    def send_chunk(c):
        for q in range(GROUP):
            k = c * GROUP + q
            for h in range(per_half):
                part = runs[tile_run[k], tile_row[k], :, h * piece:(h + 1) * piece]
                xs[h, k] = part.astype(xs.dtype)
        for h in range(per_half):

            @pl.when(sub * per_half + h != op)
            def _():
                x_copy(h, c).start()

    def add_chunk(c):
        for slot in range(op_count - 1):
            x_wait(slot, c)
        own = pl.ds(pl.multiple_of(lax.rem(op, per_half) * piece, piece), piece)
        for q in range(GROUP):
            k = c * GROUP + q
            total = runs[tile_run[k], tile_row[k], :, own]
            for slot in range(op_count - 1):
                total += xr[slot, k].astype(jnp.float32)
            xr[0, k] = total.astype(xr.dtype)
        t_copy(c).start()

    def pass_on(c, has_in, has_out, to):
        @pl.when(has_in)
        def _():
            z_copy(c, to).wait_recv()

        @pl.when(has_out)
        def _():
            @pl.when(c >= SLOTS)
            def _():
                z_copy(c - SLOTS, to).wait_send()

            @pl.when(has_in)
            def _():
                zout[lax.rem(c, SLOTS)] = (
                    xr[0, chunk_tiles(c)].astype(jnp.float32)
                    + zin[chunk_tiles(c)].astype(jnp.float32)
                ).astype(zout.dtype)

            @pl.when(jnp.logical_not(has_in))
            def _():
                zout[lax.rem(c, SLOTS)] = xr[0, chunk_tiles(c)]

            z_copy(c, to).start()

    def finish(has_in, has_got, has_out, to):
        def tile(j, row):
            return jnp.minimum(first[blk * blocks + j] + row, chunks * GROUP - 1)

        steps = half // TILE

        @pl.when(has_in)
        def _():
            @pl.loop(0, blocks)
            def _(j):
                for r in range(steps):
                    stage[j, r * TILE:(r + 1) * TILE] = zin[tile(j, (1 - sub) * steps + r)]
                out_copy(j).start()

        @pl.loop(0, blocks)
        def _(j):
            @pl.when(has_got)
            def _():
                out_copy(j).wait_recv()

            t = blk * blocks + j
            for r in range(steps):
                row = sub * steps + r
                total = xr[0, tile(j, row)].astype(jnp.float32)
                total += jnp.where(has_in, zin[tile(j, row)].astype(jnp.float32), 0.0)
                given = got[j, r * TILE:(r + 1) * TILE].astype(jnp.float32)
                total += jnp.where(has_got, given, 0.0)
                shape = total.shape
                keep = (
                    lax.broadcasted_iota(jnp.int32, shape, 0) + row * TILE < row_counts[t]
                ) & (lax.broadcasted_iota(jnp.int32, shape, 1) + op * piece < col_counts[t])
                out[j, r * TILE:(r + 1) * TILE] = jnp.where(keep, total, 0.0)

        @pl.when(has_in)
        def _():
            @pl.loop(0, blocks)
            def _(j):
                out_copy(j).wait_send()

        @pl.when(has_out)
        def _():
            @pl.loop(chunks - SLOTS, chunks)
            def _(c):
                z_copy(c, to).wait_send()

    @pl.when(owner)
    def _():
        if op_count > 2:
            pl.loop(0, chunks)(send_chunk)

        @pl.loop(0, chunks + SKEW * (count - 1))
        def _(i):
            @pl.when(i < chunks)
            def _():
                add_chunk(i)

            c = i - SKEW * blk

            @pl.when((c >= 0) & (c < chunks))
            def _():
                pass_on(c, has_low, has_high, blk + 1)

        finish(has_low, has_high, has_high, blk + 1)

        @pl.loop(0, chunks)
        def _(c):
            t_copy(c).wait_send()

    @pl.when(jnp.logical_not(owner))
    def _():
        @pl.loop(0, chunks + AHEAD)
        def _(i):
            @pl.when(i < chunks)
            def _():
                send_chunk(i)

            @pl.when(i >= AHEAD)
            def _():
                t_copy(i - AHEAD).wait_recv()
                pass_on(i - AHEAD, has_high, has_low, blk - 1)

        finish(has_high, has_low, has_low, blk - 1)

    @pl.loop(0, pairs)
    def _(p):
        done_copy(p).wait_send()

    for h in range(per_half):

        @pl.when(sub * per_half + h != op)
        def _():
            @pl.loop(0, chunks)
            def _(c):
                x_copy(h, c).wait_send()


def local(wavefunction, left_ops, right_ops, src_local, dst_dev, dst_local, row_counts, col_counts):
    blocks, half, width = wavefunction.shape
    rows = 2 * half
    pairs = left_ops.shape[0]
    count, op_count = lax.axis_size("blk"), lax.axis_size("op")
    piece = width // op_count
    targets = count * blocks
    most = (targets * rows // 2 + targets * (TILE - 1)) // TILE
    chunks = -(-most // GROUP)
    packed = chunks * GROUP
    dma = pltpu.SemaphoreType.DMA
    bf16 = jnp.bfloat16
    return pl.pallas_call(
        functools.partial(kernel, count, op_count, chunks),
        out_shape=jax.ShapeDtypeStruct((blocks, half, piece), jnp.float32),
        in_specs=[pl.BlockSpec(memory_space=pl.ANY)] * 3 + [pl.BlockSpec(memory_space=pltpu.SMEM)] * 5,
        out_specs=pl.BlockSpec(memory_space=pltpu.VMEM),
        scratch_shapes=[
            pltpu.VMEM((blocks, rows, width), bf16),
            pltpu.VMEM((pairs, rows, width), bf16),
            pltpu.VMEM((pairs, half, width), bf16),
            pltpu.VMEM((pairs + 1, rows // TILE, TILE, width // 2), jnp.float32),
            pltpu.VMEM((op_count // 2, packed, TILE, piece), bf16),
            pltpu.VMEM((op_count - 1, packed, TILE, piece), bf16),
            pltpu.VMEM((packed, TILE, piece), bf16),
            pltpu.VMEM((SLOTS, GROUP, TILE, piece), bf16),
            pltpu.VMEM((blocks, half, piece), bf16),
            pltpu.VMEM((blocks, half, piece), bf16),
            pltpu.SMEM((pairs,), jnp.int32),
            pltpu.SMEM((targets,), jnp.int32),
            pltpu.SMEM((targets,), jnp.int32),
            pltpu.SMEM((targets + 1,), jnp.int32),
            pltpu.SMEM((chunks * GROUP + 1,), jnp.int32),
            pltpu.SMEM((chunks * GROUP + 1,), jnp.int32),
            pltpu.SMEM((chunks * GROUP,), jnp.int32),
            dma,
            dma((pairs,)),
            dma((pairs,)),
            dma,
            dma,
            dma((pairs,)),
            dma((pairs,)),
            dma((op_count // 2, chunks)),
            dma((op_count - 1, chunks)),
            dma((chunks,)),
            dma((chunks,)),
            dma((chunks,)),
            dma((chunks,)),
            dma((blocks,)),
            dma((blocks,)),
        ],
        compiler_params=pltpu.CompilerParams(
            collective_id=0, has_side_effects=True, vmem_limit_bytes=60 * 2**20
        ),
        cost_estimate=pl.CostEstimate(
            flops=4 * pairs * half * width * width * 2,
            bytes_accessed=2 * left_ops.size * 2 + 2 * wavefunction.size,
            transcendentals=0,
        ),
    )(
        wavefunction, left_ops, right_ops, src_local, dst_dev.reshape(pairs), dst_local,
        row_counts, col_counts,
    )


def solution(mesh):
    placed = (
        P(("groups", "blk"), "sub", None),
        P(("groups", "blk", "op"), "sub", None),
        P(("groups", "blk", "op"), "sub", None),
        P(("groups", "blk", "op")),
        P(("groups", "blk", "op"), None),
        P(("groups", "blk", "op")),
        P("groups"),
        P("groups"),
    )
    return jax.shard_map(
        local,
        mesh=mesh,
        in_specs=placed,
        out_specs=P(("groups", "blk"), "sub", "op"),
        check_vma=False,
    )
```

```python
import functools

import jax
import jax.numpy as jnp
from jax import lax
from jax.experimental import pallas as pl
from jax.experimental.pallas import tpu as pltpu
from jax.sharding import PartitionSpec as P

MESH = pl.DeviceIdType.MESH


TILE = 16
GROUP = 8
SKEW = 6
AHEAD = 20


def kernel(
    count, op_count, chunks,
    wave_hbm, left_hbm, right_hbm, src, dst_dev, dst_local, row_counts, col_counts, out,
    wave, done, right, runs, xs, xr, zin, zout, stage, got, prev, last, tiles, first, tile_of, tile_row, tile_run,
    local_sem, left_sem, own_sem, wave_send, wave_recv, done_send, done_recv,
    x_send, x_recv, t_send, t_recv, z_send, z_recv, out_send, out_recv,
):
    blk, op, sub = lax.axis_index("blk"), lax.axis_index("op"), lax.axis_index("sub")
    pairs, half, width = right.shape
    blocks = wave.shape[0]
    targets = count * blocks
    piece = out.shape[2]
    per_half = op_count // 2
    owner = op // per_half == sub
    has_low, has_high = blk > 0, blk < count - 1
    mine = pl.ds(pl.multiple_of(sub * half, half), half)

    wave_local = pltpu.make_async_copy(wave_hbm, wave.at[:, mine], local_sem)
    wave_local.start()

    def left_copy(p):
        return pltpu.make_async_copy(left_hbm.at[p], done.at[p, mine], left_sem.at[p])

    def right_copy(p):
        return pltpu.make_async_copy(right_hbm.at[p], right.at[p], own_sem.at[p])

    @pl.loop(0, pairs)
    def _(p):
        left_copy(p).start()

    @pl.loop(0, pairs)
    def _(p):
        right_copy(p).start()

    barrier = pltpu.get_barrier_semaphore()
    pl.semaphore_signal(barrier, inc=1, device_id={"sub": 1 - sub}, device_id_type=MESH)
    for step in range(1, op_count):
        pl.semaphore_signal(
            barrier, inc=1, device_id={"op": lax.rem(op + step, op_count)}, device_id_type=MESH
        )

    @pl.when(has_low)
    def _():
        pl.semaphore_signal(barrier, inc=1, device_id={"blk": blk - 1}, device_id_type=MESH)

    @pl.when(has_high)
    def _():
        pl.semaphore_signal(barrier, inc=1, device_id={"blk": blk + 1}, device_id_type=MESH)

    pl.semaphore_wait(barrier, op_count + has_low.astype(jnp.int32) + has_high.astype(jnp.int32))

    wave_copy = pltpu.make_async_remote_copy(
        src_ref=wave_hbm, dst_ref=wave.at[:, mine], send_sem=wave_send, recv_sem=wave_recv,
        device_id={"sub": 1 - sub}, device_id_type=MESH,
    )
    wave_copy.start()

    def done_copy(p):
        return pltpu.make_async_remote_copy(
            src_ref=done.at[p, mine], dst_ref=done.at[p, mine],
            send_sem=done_send.at[p], recv_sem=done_recv.at[p],
            device_id={"sub": 1 - sub}, device_id_type=MESH,
        )

    goals = [dst_dev[p] * blocks + dst_local[p] for p in range(pairs)]
    for p in range(pairs):
        found = jnp.int32(0)
        for q in range(p):
            found = jnp.where(goals[q] == goals[p], q + 1, found)
        prev[p] = found

    first[0] = 0

    @pl.loop(0, targets)
    def _(t):
        found = jnp.int32(0)
        for p in range(pairs):
            found = jnp.where(goals[p] == t, p + 1, found)
        last[t] = found
        tiles[t] = lax.div(row_counts[t] + (TILE - 1), TILE)
        first[t + 1] = first[t] + tiles[t]

    gap = chunks * GROUP - first[targets]

    @pl.loop(targets // 2, targets + 1)
    def _(t):
        first[t] = first[t] + gap

    tile_of[0] = 0
    tile_row[0] = 0

    @pl.loop(0, chunks * GROUP)
    def _(k):
        t, r = tile_of[k], tile_row[k]
        over = k + 1 >= first[t + 1]
        tile_of[k + 1] = jnp.where(over, jnp.minimum(t + 1, targets - 1), t)
        tile_row[k + 1] = jnp.where(over, 0, jnp.minimum(r + 1, jnp.maximum(tiles[t] - 1, 0)))
        tile_run[k] = last[t]

    runs[0] = jnp.zeros(runs.shape[1:], jnp.float32)

    wave_local.wait()
    wave_copy.wait()

    @pl.loop(0, blocks)
    def _(j):
        at = blk * blocks + j
        shape = wave.shape[1:]
        keep = (lax.broadcasted_iota(jnp.int32, shape, 0) < row_counts[at]) & (
            lax.broadcasted_iota(jnp.int32, shape, 1) < col_counts[at]
        )
        wave[j] = jnp.where(keep, wave[j].astype(jnp.float32), 0.0).astype(wave.dtype)

    @pl.loop(0, pairs)
    def _(p):
        left_copy(p).wait()
        part = jnp.dot(done[p, mine], wave[src[p]], preferred_element_type=jnp.float32)
        done[p, mine] = part.astype(done.dtype)
        done_copy(p).start()

    @pl.loop(0, pairs)
    def _(p):
        right_copy(p).wait()
        done_copy(p).wait_recv()
        for side in range(2):
            product = lax.dot_general(
                done[p, side * half:(side + 1) * half], right[p], (((1,), (1,)), ((), ())),
                preferred_element_type=jnp.float32,
            ).astype(jnp.bfloat16)
            part = product.astype(jnp.float32).reshape((half // TILE,) + runs.shape[2:])
            at = pl.ds(side * (half // TILE), half // TILE)
            runs[p + 1, at] = part + runs[prev[p], at]

    def chunk_tiles(c):
        return pl.ds(c * GROUP, GROUP)

    def x_copy(h, c):
        to = sub * per_half + h
        slot = lax.rem(op - to + op_count - 1 + op_count, op_count)
        return pltpu.make_async_remote_copy(
            src_ref=xs.at[h, chunk_tiles(c)], dst_ref=xr.at[slot, chunk_tiles(c)],
            send_sem=x_send.at[h, c], recv_sem=x_recv.at[slot, c],
            device_id={"op": to}, device_id_type=MESH,
        )

    def x_wait(slot, c):
        pltpu.make_async_remote_copy(
            src_ref=xs.at[0, chunk_tiles(c)], dst_ref=xr.at[slot, chunk_tiles(c)],
            send_sem=x_send.at[0, c], recv_sem=x_recv.at[slot, c],
            device_id={"op": op}, device_id_type=MESH,
        ).wait_recv()

    def t_copy(c):
        return pltpu.make_async_remote_copy(
            src_ref=xr.at[0, chunk_tiles(c)], dst_ref=xr.at[0, chunk_tiles(c)],
            send_sem=t_send.at[c], recv_sem=t_recv.at[c],
            device_id={"sub": 1 - sub}, device_id_type=MESH,
        )

    def z_copy(c, to):
        return pltpu.make_async_remote_copy(
            src_ref=zout.at[chunk_tiles(c)], dst_ref=zin.at[chunk_tiles(c)],
            send_sem=z_send.at[c], recv_sem=z_recv.at[c],
            device_id={"blk": to}, device_id_type=MESH,
        )

    def out_copy(j):
        return pltpu.make_async_remote_copy(
            src_ref=stage.at[j], dst_ref=got.at[j], send_sem=out_send.at[j], recv_sem=out_recv.at[j],
            device_id={"sub": 1 - sub}, device_id_type=MESH,
        )

    def send_chunk(c):
        for q in range(GROUP):
            k = c * GROUP + q
            for h in range(per_half):
                part = runs[tile_run[k], tile_row[k], :, h * piece:(h + 1) * piece]
                xs[h, k] = part.astype(xs.dtype)
        for h in range(per_half):

            @pl.when(sub * per_half + h != op)
            def _():
                x_copy(h, c).start()

    def add_chunk(c):
        for slot in range(op_count - 1):
            x_wait(slot, c)
        own = pl.ds(pl.multiple_of(lax.rem(op, per_half) * piece, piece), piece)
        for q in range(GROUP):
            k = c * GROUP + q
            total = runs[tile_run[k], tile_row[k], :, own]
            for slot in range(op_count - 1):
                total += xr[slot, k].astype(jnp.float32)
            xr[0, k] = total.astype(xr.dtype)
        t_copy(c).start()

    def turn(i):
        return jnp.where(lax.rem(i, 2) == 0, chunks - 1 - i // 2, i // 2)

    share = blocks * 2 * half // TILE

    def goes_up(c, at):
        kept = (c + 1) * GROUP > chunks * GROUP - (count - 1 - at) * share
        return (at >= 0) & (at < count - 1) & ((at + 1 < count // 2) | kept)

    def goes_down(c, at):
        return (at > 0) & (at < count) & ((at > count // 2) | (c * GROUP < at * share))

    def pass_on(c, has_in, has_out, to):
        @pl.when(has_in)
        def _():
            z_copy(c, to).wait_recv()

        @pl.when(has_out)
        def _():
            @pl.when(has_in)
            def _():
                zout[chunk_tiles(c)] = (
                    xr[0, chunk_tiles(c)].astype(jnp.float32)
                    + zin[chunk_tiles(c)].astype(jnp.float32)
                ).astype(zout.dtype)

            @pl.when(jnp.logical_not(has_in))
            def _():
                zout[chunk_tiles(c)] = xr[0, chunk_tiles(c)]

            z_copy(c, to).start()

    def finish(has_in, has_got, sent, to):
        def tile(j, row):
            return jnp.minimum(first[blk * blocks + j] + row, chunks * GROUP - 1)

        steps = half // TILE

        @pl.when(has_in)
        def _():
            @pl.loop(0, blocks)
            def _(j):
                for r in range(steps):
                    stage[j, r * TILE:(r + 1) * TILE] = zin[tile(j, (1 - sub) * steps + r)]
                out_copy(j).start()

        @pl.loop(0, blocks)
        def _(j):
            @pl.when(has_got)
            def _():
                out_copy(j).wait_recv()

            t = blk * blocks + j
            for r in range(steps):
                row = sub * steps + r
                total = xr[0, tile(j, row)].astype(jnp.float32)
                total += jnp.where(has_in, zin[tile(j, row)].astype(jnp.float32), 0.0)
                given = got[j, r * TILE:(r + 1) * TILE].astype(jnp.float32)
                total += jnp.where(has_got, given, 0.0)
                shape = total.shape
                keep = (
                    lax.broadcasted_iota(jnp.int32, shape, 0) + row * TILE < row_counts[t]
                ) & (lax.broadcasted_iota(jnp.int32, shape, 1) + op * piece < col_counts[t])
                out[j, r * TILE:(r + 1) * TILE] = jnp.where(keep, total, 0.0)

        @pl.when(has_in)
        def _():
            @pl.loop(0, blocks)
            def _(j):
                out_copy(j).wait_send()

        @pl.loop(0, chunks)
        def _(c):
            @pl.when(sent(c, blk))
            def _():
                z_copy(c, to).wait_send()

    @pl.when(owner)
    def _():
        if op_count > 2:
            pl.loop(0, chunks)(lambda i: send_chunk(turn(i)))

        @pl.loop(0, chunks + SKEW * (count - 1))
        def _(i):
            @pl.when(i < chunks)
            def _():
                add_chunk(turn(i))

            back = i - SKEW * blk

            @pl.when((back >= 0) & (back < chunks))
            def _():
                c = turn(back)
                pass_on(c, goes_up(c, blk - 1), goes_up(c, blk), blk + 1)

        finish(has_low, has_high, goes_up, blk + 1)

        @pl.loop(0, chunks)
        def _(c):
            t_copy(c).wait_send()

    @pl.when(jnp.logical_not(owner))
    def _():
        @pl.loop(0, chunks + AHEAD)
        def _(i):
            @pl.when(i < chunks)
            def _():
                send_chunk(turn(i))

            @pl.when(i >= AHEAD)
            def _():
                c = turn(i - AHEAD)
                t_copy(c).wait_recv()
                pass_on(c, goes_down(c, blk + 1), goes_down(c, blk), blk - 1)

        finish(has_high, has_low, goes_down, blk - 1)

    @pl.loop(0, pairs)
    def _(p):
        done_copy(p).wait_send()

    for h in range(per_half):

        @pl.when(sub * per_half + h != op)
        def _():
            @pl.loop(0, chunks)
            def _(c):
                x_copy(h, c).wait_send()


def local(wavefunction, left_ops, right_ops, src_local, dst_dev, dst_local, row_counts, col_counts):
    blocks, half, width = wavefunction.shape
    rows = 2 * half
    pairs = left_ops.shape[0]
    count, op_count = lax.axis_size("blk"), lax.axis_size("op")
    piece = width // op_count
    targets = count * blocks
    most = (targets * rows // 2 + targets * (TILE - 1)) // TILE
    chunks = -(-most // GROUP)
    packed = chunks * GROUP
    dma = pltpu.SemaphoreType.DMA
    bf16 = jnp.bfloat16
    return pl.pallas_call(
        functools.partial(kernel, count, op_count, chunks),
        out_shape=jax.ShapeDtypeStruct((blocks, half, piece), jnp.float32),
        in_specs=[pl.BlockSpec(memory_space=pl.ANY)] * 3 + [pl.BlockSpec(memory_space=pltpu.SMEM)] * 5,
        out_specs=pl.BlockSpec(memory_space=pltpu.VMEM),
        scratch_shapes=[
            pltpu.VMEM((blocks, rows, width), bf16),
            pltpu.VMEM((pairs, rows, width), bf16),
            pltpu.VMEM((pairs, half, width), bf16),
            pltpu.VMEM((pairs + 1, rows // TILE, TILE, width // 2), jnp.float32),
            pltpu.VMEM((op_count // 2, packed, TILE, piece), bf16),
            pltpu.VMEM((op_count - 1, packed, TILE, piece), bf16),
            pltpu.VMEM((packed, TILE, piece), bf16),
            pltpu.VMEM((packed, TILE, piece), bf16),
            pltpu.VMEM((blocks, half, piece), bf16),
            pltpu.VMEM((blocks, half, piece), bf16),
            pltpu.SMEM((pairs,), jnp.int32),
            pltpu.SMEM((targets,), jnp.int32),
            pltpu.SMEM((targets,), jnp.int32),
            pltpu.SMEM((targets + 1,), jnp.int32),
            pltpu.SMEM((chunks * GROUP + 1,), jnp.int32),
            pltpu.SMEM((chunks * GROUP + 1,), jnp.int32),
            pltpu.SMEM((chunks * GROUP,), jnp.int32),
            dma,
            dma((pairs,)),
            dma((pairs,)),
            dma,
            dma,
            dma((pairs,)),
            dma((pairs,)),
            dma((op_count // 2, chunks)),
            dma((op_count - 1, chunks)),
            dma((chunks,)),
            dma((chunks,)),
            dma((chunks,)),
            dma((chunks,)),
            dma((blocks,)),
            dma((blocks,)),
        ],
        compiler_params=pltpu.CompilerParams(
            collective_id=0, has_side_effects=True, vmem_limit_bytes=60 * 2**20
        ),
        cost_estimate=pl.CostEstimate(
            flops=4 * pairs * half * width * width * 2,
            bytes_accessed=2 * left_ops.size * 2 + 2 * wavefunction.size,
            transcendentals=0,
        ),
    )(
        wavefunction, left_ops, right_ops, src_local, dst_dev.reshape(pairs), dst_local,
        row_counts, col_counts,
    )


def solution(mesh):
    placed = (
        P(("groups", "blk"), "sub", None),
        P(("groups", "blk", "op"), "sub", None),
        P(("groups", "blk", "op"), "sub", None),
        P(("groups", "blk", "op")),
        P(("groups", "blk", "op"), None),
        P(("groups", "blk", "op")),
        P("groups"),
        P("groups"),
    )
    return jax.shard_map(
        local,
        mesh=mesh,
        in_specs=placed,
        out_specs=P(("groups", "blk"), "sub", "op"),
        check_vma=False,
    )
```
